32 devices in a mesh: groups: 2 (over y), lon: 4 (over z), lat: 2 (over core), member: 2 (over x).
Axes of the slice: x: 2, y: 2, z: 4, core: 2. Of those that a mesh axis runs over, the one named last changes fastest.
Arguments:
- latent: bfloat16 [4, 32, 256, 256], P(('groups', 'member'), 'lat', 'lon'), parts along dimension 0, may hold values from -6 to 6
- target: float32 [64, 256, 72], P(('groups', 'lat'), 'lon'), parts along dimension 0, may hold values from -6 to 6
- quadrature: bfloat16 [4, 32, 5, 17], replicated, may hold values from -0.625 to 0.625
- widths: int32 [32], replicated, may hold values from 1 to 8, as said below
- conv_weight: bfloat16 [1024, 256], replicated, may hold values from -0.1875 to 0.1875
- output_weight: bfloat16 [256, 72], replicated, may hold values from -0.375 to 0.375
Outputs:
- grad_latent: bfloat16 [4, 32, 256, 256], P(('groups', 'member'), 'lat', 'lon'), parts along dimension 0
- grad_conv: float32 [2048, 256], P('groups'), parts along dimension 0
- grad_out: float32 [512, 72], P('groups'), parts along dimension 0
The draws below stay inside these ranges and needn't reach their ends.
There are 2 independent parts, one for each index of `groups`. The reference program is written for one: setup_inputs(seed, part) draws one part's arguments, and reference() takes and returns one part's arrays. A program takes and returns all parts, laid end to end along the dimension named above; an argument that names none is the same for every part. Nothing has to cross between parts.
Inputs may be any that keep to these rules, and one draw needn't show every extreme that they name: widths[0] equals 8 and the last row's width is 1.
All inputs are finite; a program needn't handle non-finite values.
Results may differ from the reference program's by a relative error of at most 0.012.
Values may be sent and summed in bfloat16 or wider, within the bound.
A program may use at most 64 MiB of HBM per device.

```python
import math
import jax
import jax.numpy as jnp
from jax import lax

C = 256
FIELDS = 72
K = 4
RAD = 2
W_MAX = 8
NLAT = 32
NLON = 256
ENSEMBLE_SIZE = 2


def draw_widths(key, part):
    key = jax.random.fold_in(key, 11)
    row_index = jnp.arange(NLAT)
    base_width = W_MAX - (W_MAX - 1) * row_index // max(NLAT - 1, 1)
    jitter = jax.random.randint(key, (NLAT,), 0, 2)
    width_rows = jnp.clip(base_width - jitter, 1, W_MAX)
    return jnp.where(row_index == 0, W_MAX, width_rows).astype(jnp.int32)


def steps_of(rng, dims, shards, least, top_value):
    level, own = 1.0, jax.random.fold_in(rng, 6)
    for position, shards_of in shards:
        draws = jnp.exp(jax.random.uniform(jax.random.fold_in(own, position), (shards_of,), jnp.float32, least / len(shards), top_value / len(shards)))
        level = level * jnp.repeat(draws, dims[position] // shards_of).reshape([-1 if axis == position else 1 for axis in range(len(dims))])
    return level


def normal_values(stream_key, extent, width, reach, shards=(), kind=jnp.bfloat16):
    level = steps_of(stream_key, extent, shards, -0.22, 0.18) if shards else 1.0
    entries = jax.random.normal(stream_key, extent, jnp.float32) * width * level
    return jnp.minimum(jnp.maximum(entries, -reach), reach).astype(kind)


def setup_inputs(seed: int = 0, part: int = 0) -> dict:
    seeds = jax.random.split(jax.random.key(seed), 7)
    part_splits = jax.random.split(jax.random.fold_in(seeds[6], part), 7)
    return {
        "latent": normal_values(part_splits[0], (ENSEMBLE_SIZE, NLAT, NLON, C), 1.0, 6.0, ((0, 2), (1, 2), (2, 4))),
        "target": normal_values(part_splits[1], (NLAT, NLON, FIELDS), 1.0, 6.0, ((0, 2), (1, 4)), jnp.float32),
        "quadrature": normal_values(seeds[2], (K, NLAT, 2 * RAD + 1, 2 * W_MAX + 1), ((2 * RAD + 1) * (2 * W_MAX + 1)) ** -0.5, 0.625),
        "widths": draw_widths(jax.random.fold_in(seeds[6], 71), part),
        "conv_weight": normal_values(seeds[4], (K * C, C), (K * C) ** -0.5, 0.1875),
        "output_weight": normal_values(seeds[5], (C, FIELDS), C ** -0.5, 0.375),
    }


smoothing = 0.1

def softened_slope(difference):
    return difference / jnp.sqrt(difference * difference + smoothing * smoothing)

def masked_filter(quadrature, widths):
    tap_count = quadrature.shape[3]
    half_taps = tap_count // 2
    offsets = jnp.abs(jnp.arange(tap_count) - half_taps)
    keep_mask = (offsets[None, :] <= widths[:, None]).astype(quadrature.dtype)
    return quadrature * keep_mask[None, :, None, :]

def extend_rim(field_in, radius, half_taps):
    wrapped = jnp.concatenate([field_in[:, -half_taps:], field_in, field_in[:, :half_taps]], axis=1)
    pad_spec = [(radius, radius)] + [(0, 0)] * (field_in.ndim - 1)
    return jnp.pad(wrapped, pad_spec)

def basis_of(field_in, psi):
    extended = extend_rim(field_in, RAD, W_MAX)
    accum_sum = jnp.zeros((NLAT, NLON, K, C), jnp.float32)
    for lat_off in range(2 * RAD + 1):
        for lon_off in range(2 * W_MAX + 1):
            coeff_rows = psi[:, :, lat_off, lon_off].T.astype(jnp.float32)[:, None, :, None]
            window = extended[lat_off:lat_off + NLAT, lon_off:lon_off + NLON, None, :].astype(jnp.float32)
            accum_sum = accum_sum + coeff_rows * window
    return accum_sum.astype(jnp.bfloat16)

def adjoint_of(grad_cells, psi):
    extended = extend_rim(grad_cells, RAD, W_MAX)
    psi_padded = jnp.pad(psi, ((0, 0), (RAD, RAD), (0, 0), (0, 0)))
    accum_sum = jnp.zeros((NLAT, NLON, C), jnp.float32)
    for lat_off in range(2 * RAD + 1):
        row_from = 2 * RAD - lat_off
        for lon_off in range(2 * W_MAX + 1):
            col_from = 2 * W_MAX - lon_off
            coeff_rows = psi_padded[:, row_from:row_from + NLAT, lat_off, lon_off].T.astype(jnp.float32)[:, None, :, None]
            window = extended[row_from:row_from + NLAT, col_from:col_from + NLON].astype(jnp.float32)
            accum_sum = accum_sum + lax.optimization_barrier(jnp.sum(coeff_rows * window, axis=2))
    return accum_sum

def forward_parts(field_in, psi, conv_weight, output_weight):
    cell_count = NLAT * NLON
    basis_all = basis_of(field_in, psi).reshape(cell_count, K * C)
    hidden = jnp.dot(basis_all, conv_weight, preferred_element_type=jnp.float32)
    blended_rows = (field_in.reshape(cell_count, C).astype(jnp.float32) + jax.nn.gelu(hidden)).astype(jnp.bfloat16)
    return (basis_all, hidden, blended_rows)

def reference(latent, target, quadrature, widths, conv_weight, output_weight):
    psi = masked_filter(quadrature, widths)
    cell_count = NLAT * NLON

    def single_forward(field_in):
        basis_all, hidden, blended_rows = forward_parts(field_in, psi, conv_weight, output_weight)
        return jnp.dot(blended_rows, output_weight, preferred_element_type=jnp.float32).astype(jnp.bfloat16)
    predicted_state = lax.map(single_forward, latent).astype(jnp.float32)
    observed_rows = target.reshape(cell_count, FIELDS)
    pairwise_sum = jnp.zeros_like(predicted_state)
    for second_member in range(ENSEMBLE_SIZE):
        pairwise_sum = pairwise_sum + softened_slope(predicted_state - predicted_state[second_member][None])
    prediction_gradient = (softened_slope(predicted_state - observed_rows[None]) - pairwise_sum / (ENSEMBLE_SIZE - 1)).astype(jnp.bfloat16)

    def backward_one(running, inputs):
        field_in, grad_pred = inputs
        basis_all, hidden, blended_rows = forward_parts(field_in, psi, conv_weight, output_weight)
        up_grad = jnp.dot(grad_pred, output_weight.T, preferred_element_type=jnp.float32)
        hid_grad = jax.vjp(jax.nn.gelu, hidden)[1](up_grad)[0].astype(jnp.bfloat16)
        conv_sum = running[0] + jnp.dot(basis_all.T, hid_grad, preferred_element_type=jnp.float32)
        out_sum = running[1] + jnp.dot(blended_rows.T, grad_pred, preferred_element_type=jnp.float32)
        basis_grad = jnp.dot(hid_grad, conv_weight.T, preferred_element_type=jnp.float32).astype(jnp.bfloat16)
        basis_grad = basis_grad.reshape(NLAT, NLON, K, C)
        grad_in = (up_grad.reshape(NLAT, NLON, C) + adjoint_of(basis_grad, psi)).astype(jnp.bfloat16)
        return ((conv_sum, out_sum), grad_in)
    start_sums = (jnp.zeros((K * C, C), jnp.float32), jnp.zeros((C, FIELDS), jnp.float32))
    (conv_sum, out_sum), grad_latent = lax.scan(backward_one, start_sums, (latent, prediction_gradient))
    norm_scale = 1.0 / math.sqrt(ENSEMBLE_SIZE * NLAT * NLON)
    return (grad_latent, conv_sum * norm_scale, out_sum * norm_scale)
```

```python
import functools
import math

import jax
import jax.numpy as jnp
from jax import lax
from jax.experimental import pallas as pl
from jax.experimental.pallas import tpu as pltpu
from jax.sharding import PartitionSpec as P

smoothing = 0.1
MESH = pl.DeviceIdType.MESH
f32 = jnp.float32
bf16 = jnp.bfloat16
CHUNKS = 4


def slope(d):
    return d * lax.rsqrt(d * d + smoothing * smoothing)


def dims_of(rows, cols, taps_lat, half):
    pitch = cols + 2 * half
    slots = rows + taps_lat - 1
    window = -(-(16 + taps_lat * pitch) // 128) * 128
    return pitch, slots, window, (rows - 1) * pitch + window


def kernel(sizes, lat_ref, tgt_ref, base_ref, cw_ref, ow_ref, gl_ref, gc_ref, go_ref,
           T, X, G, basis, BG, DG, mixed, F, FR, wo, pg, hg, GF, GB, GA,
           SL, SR, RL, RR, RC, SL2, SR2, SC2, QL, QR, QC, QLd, QRd, R1, R2, R3,
           hs, hr, fs, fr, as_, ar, s1s, s1r, s2s, s2r, s3s, s3r, a3s, a3r, a2s, a2r, a1s, a1r):
    rows, cols, C, K, taps_lat, half, L, M, fields, scale = sizes
    radius = taps_lat // 2
    pitch, slots, window, span = dims_of(rows, cols, taps_lat, half)
    n = rows * cols
    per = rows // CHUNKS
    cn = per * cols
    lat = lax.axis_index("lat")
    lon = lax.axis_index("lon")
    mem = lax.axis_index("member")
    other = 1 - lat
    right = lax.rem(lon + 1, L)
    left = lax.rem(lon + L - 1, L)
    hh = radius * half

    def rcopy(src, dst, ss, rs, dev):
        return pltpu.make_async_remote_copy(
            src_ref=src, dst_ref=dst, send_sem=ss, recv_sem=rs, device_id=dev, device_id_type=MESH)

    barrier = pltpu.get_barrier_semaphore()
    peers = [{"lat": other}, {"lat": other, "lon": left}, {"lat": other, "lon": right}]
    peers += [{"lon": lax.rem(lon + d, L)} for d in range(1, L)]
    peers += [{"member": lax.rem(mem + d, M)} for d in range(1, M)]
    for dev in peers:
        pl.semaphore_signal(barrier, inc=1, device_id=dev, device_id_type=MESH)

    lat3 = lat_ref[...].astype(f32).reshape(rows, cols, C)
    SL[...] = lat3[:, :half].reshape(rows * half, C).astype(bf16)
    SR[...] = lat3[:, cols - half:].reshape(rows * half, C).astype(bf16)
    zero_halo = jnp.zeros((hh, C), bf16)
    edge = pl.multiple_of(lat * (hh + rows * half), 16)
    RL[pl.ds(edge, hh), :] = zero_halo
    RR[pl.ds(edge, hh), :] = zero_halo
    pl.semaphore_wait(barrier, len(peers))

    near = pl.multiple_of(other * (rows - radius) * half, 16)
    far = pl.multiple_of(lat * 0 + (1 - other) * (hh + rows * half), 16)
    nearrow = pl.multiple_of(other * (rows - radius) * cols, 16)
    inner = pl.ds(hh, rows * half)
    halo = [
        rcopy(SL, RR.at[inner], hs.at[0], hr.at[0], {"lon": left}),
        rcopy(SR, RL.at[inner], hs.at[1], hr.at[1], {"lon": right}),
        rcopy(SL.at[pl.ds(near, hh)], RR.at[pl.ds(far, hh)], hs.at[2], hr.at[2], {"lat": other, "lon": left}),
        rcopy(SR.at[pl.ds(near, hh)], RL.at[pl.ds(far, hh)], hs.at[3], hr.at[3], {"lat": other, "lon": right}),
        rcopy(lat_ref.at[pl.ds(nearrow, radius * cols)], RC, hs.at[4], hr.at[4], {"lat": other}),
    ]
    for c in halo:
        c.start()

    def build(i, carry):
        rowsb = base_ref[pl.ds(pl.multiple_of(i * 8, 8), 8), :]
        for k in range(K):
            line = jnp.broadcast_to(rowsb[k:k + 1, :], (cols, window))
            T[i, k * cols:(k + 1) * cols, :] = pltpu.roll(line, 0, 1, stride=1, stride_axis=0).astype(bf16)
        return carry
    lax.fori_loop(0, rows, build, 0)

    G[...] = jnp.zeros(G.shape, f32)
    wo[...] = jnp.zeros(wo.shape, bf16)
    wo[:, :fields] = ow_ref[...]
    pg[...] = jnp.zeros(pg.shape, bf16)
    X[pl.ds(16 + slots * pitch, span - 16 - slots * pitch), :] = jnp.zeros((span - 16 - slots * pitch, C), bf16)
    for r in range(rows):
        X[16 + pitch * (r + radius):16 + pitch * (r + radius) + cols, :] = lat_ref[r * cols:(r + 1) * cols, :]
    zrow = jnp.zeros((cols, C), bf16)
    for r in range(radius):
        X[pl.ds(pl.multiple_of(16 + pitch * (r + lat * (rows + radius)), 16), cols), :] = zrow
    for c in halo:
        c.wait()
    for r in range(radius):
        X[pl.ds(pl.multiple_of(16 + pitch * (r + other * (rows + radius)), 16), cols), :] = RC[r * cols:(r + 1) * cols, :]
    rl = RL[...].astype(f32)
    rr = RR[...].astype(f32)
    z8 = jnp.zeros((half, C), f32)
    X[0:16, :] = jnp.concatenate([z8, rl[0:half]], axis=0).astype(bf16)
    for r in range(slots):
        nxt = rl[(r + 1) * half:(r + 2) * half] if r + 1 < slots else z8
        X[16 + pitch * r + cols:16 + pitch * (r + 1), :] = jnp.concatenate(
            [rr[r * half:(r + 1) * half], nxt], axis=0).astype(bf16)

    c0 = math.sqrt(2 / math.pi)
    fcopies = []
    for ch in range(CHUNKS):
        def conv(ii, carry, ch=ch):
            i = ch * per + ii
            out = jnp.dot(T[i], X[pl.ds(pl.multiple_of(i * pitch, 16), window), :], preferred_element_type=f32).astype(bf16)
            for k in range(K):
                basis[pl.ds(pl.multiple_of(i * cols, 16), cols), k * C:(k + 1) * C] = out[k * cols:(k + 1) * cols]
            return carry
        lax.fori_loop(0, per, conv, 0, unroll=True)
        sl = slice(ch * cn, (ch + 1) * cn)
        h = jnp.dot(basis[sl, :], cw_ref[...], preferred_element_type=f32)
        t = jnp.tanh(c0 * (h + 0.044715 * h * h * h))
        DG[sl, :] = 0.5 * (1 + t) + 0.5 * h * (1 - t * t) * (c0 * (1 + 3 * 0.044715 * h * h))
        mx = (lat_ref[sl, :].astype(f32) + 0.5 * h * (1 + t)).astype(bf16)
        mixed[sl, :] = mx
        F[sl, :] = jnp.dot(mx, wo[...], preferred_element_type=f32).astype(bf16)
        cs = []
        for d in range(1, M):
            c = rcopy(F.at[pl.ds(ch * cn, cn)], FR.at[d - 1, pl.ds(ch * cn, cn)], fs.at[d - 1, ch], fr.at[d - 1, ch],
                      {"member": lax.rem(mem + d, M)})
            c.start()
            cs.append(c)
        fcopies.append(cs)

    for ch in range(CHUNKS):
        sl = slice(ch * cn, (ch + 1) * cn)
        mine = F[sl, :fields].astype(f32)
        first = slope(mine - tgt_ref[sl, :])
        for c in fcopies[ch]:
            c.wait()
        pair = jnp.zeros_like(mine)
        for d in range(1, M):
            pair = pair + slope(mine - FR[d - 1, sl, :fields].astype(f32))
        pg[sl, :fields] = (first - pair * (1.0 / (M - 1))).astype(bf16)
        up = lax.dot_general(pg[sl, :], wo[...], (((1,), (1,)), ((), ())), preferred_element_type=f32)
        for ii in range(per):
            r = ch * per + ii + radius
            G[16 + pitch * r:16 + pitch * r + cols, :] = up[ii * cols:(ii + 1) * cols]
        hg[sl, :] = (up * DG[sl, :]).astype(bf16)

    KC = K * C
    hc = C // 2
    total = 2 * KC + C
    tn = (((0,), (0,)), ((), ()))
    hgv = hg[...]
    for k in range(K):
        g = lax.dot_general(basis[:, k * C:(k + 1) * C], hgv, tn, preferred_element_type=f32)
        for half_id in range(2):
            part = g[:, half_id * hc:(half_id + 1) * hc]
            at = half_id * KC + k * C
            GF[at:at + C, :] = part
            GB[at:at + C, :] = part.astype(bf16)
    g = lax.dot_general(mixed[...], pg[...], tn, preferred_element_type=f32)
    GF[2 * KC:total, :] = g
    GB[2 * KC:total, :] = g.astype(bf16)

    n1 = total // 2
    n2 = n1 // M
    scatter = n2 % (16 * L) == 0
    n3 = n2 // L if scatter else n2
    o1 = pl.multiple_of(lat * n1, 16)
    o1o = pl.multiple_of(other * n1, 16)
    st1 = rcopy(GB.at[pl.ds(o1o, n1)], R1, s1s, s1r, {"lat": other})
    st1.start()

    def adjoint(first_row, last_row):
        lo, size = first_row * cols, (last_row - first_row) * cols
        BG[lo:lo + size, :] = lax.dot_general(
            hg[lo:lo + size, :], cw_ref[...], (((1,), (1,)), ((), ())), preferred_element_type=f32).astype(bf16)

        def body(i, carry):
            at = pl.ds(pl.multiple_of(i * cols, 16), cols)
            stacked = jnp.concatenate([BG[at, k * C:(k + 1) * C] for k in range(K)], axis=0)
            out = lax.dot_general(T[i], stacked, tn, preferred_element_type=f32)
            w = pl.ds(pl.multiple_of(i * pitch, 16), window)
            G[w, :] = G[w, :] + out
            return carry
        lax.fori_loop(first_row, last_row, body, 0)

    adjoint(0, rows // 2)

    st1.wait()
    v = GF[pl.ds(o1, n1), :] + R1[...].astype(f32)
    GF[pl.ds(o1, n1), :] = v
    GB[pl.ds(o1, n1), :] = v.astype(bf16)
    st2 = []
    for d in range(1, M):
        q = lax.rem(mem + d, M)
        c = rcopy(GB.at[pl.ds(pl.multiple_of(o1 + q * n2, 16), n2)], R2.at[d - 1], s2s.at[d - 1], s2r.at[d - 1], {"member": q})
        c.start()
        st2.append(c)

    adjoint(rows // 2, rows)
    for r in range(slots):
        pass
    SR2[...] = jnp.concatenate([G[16 + pitch * r + cols:16 + pitch * r + cols + half, :] for r in range(slots)], axis=0).astype(bf16)
    SL2[...] = jnp.concatenate([G[16 + pitch * r - half:16 + pitch * r, :] for r in range(slots)], axis=0).astype(bf16)
    for r in range(radius):
        SC2[r * cols:(r + 1) * cols, :] = G[pl.ds(pl.multiple_of(16 + pitch * (r + other * (rows + radius)), 16), cols), :].astype(bf16)
    beyond = pl.multiple_of(other * (hh + rows * half), 16)
    back = [
        rcopy(SR2.at[inner], QL, as_.at[0], ar.at[0], {"lon": right}),
        rcopy(SL2.at[inner], QR, as_.at[1], ar.at[1], {"lon": left}),
        rcopy(SR2.at[pl.ds(beyond, hh)], QLd, as_.at[2], ar.at[2], {"lat": other, "lon": right}),
        rcopy(SL2.at[pl.ds(beyond, hh)], QRd, as_.at[3], ar.at[3], {"lat": other, "lon": left}),
        rcopy(SC2, QC, as_.at[4], ar.at[4], {"lat": other}),
    ]
    for c in back:
        c.start()

    for c in st2:
        c.wait()
    o2 = pl.multiple_of(o1 + mem * n2, 16)
    v = GF[pl.ds(o2, n2), :]
    for d in range(1, M):
        v = v + R2[d - 1].astype(f32)
    GF[pl.ds(o2, n2), :] = v
    GB[pl.ds(o2, n2), :] = v.astype(bf16)
    st3 = []
    for d in range(1, L):
        q = lax.rem(lon + d, L)
        src = GB.at[pl.ds(pl.multiple_of(o2 + q * n3, 16), n3)] if scatter else GB.at[pl.ds(o2, n2)]
        dst = R3.at[d - 1] if scatter else R3.at[lon]
        c = rcopy(src, dst, s3s.at[d - 1], s3r.at[d - 1], {"lon": q})
        c.start()
        st3.append(c)

    for c in back:
        c.wait()
    ql = QL[...].astype(f32)
    qr = QR[...].astype(f32)
    qld = QLd[...].astype(f32)
    qrd = QRd[...].astype(f32)
    for r in range(rows):
        at = 16 + pitch * (r + radius)
        G[at:at + half, :] = G[at:at + half, :] + ql[r * half:(r + 1) * half]
        G[at + cols - half:at + cols, :] = G[at + cols - half:at + cols, :] + qr[r * half:(r + 1) * half]
    for r in range(radius):
        at = 16 + pitch * (radius + r + other * (rows - radius))
        w = pl.ds(pl.multiple_of(at, 16), cols)
        G[w, :] = G[w, :] + QC[r * cols:(r + 1) * cols, :].astype(f32)
        w = pl.ds(pl.multiple_of(at, 8), half)
        G[w, :] = G[w, :] + qld[r * half:(r + 1) * half]
        w = pl.ds(pl.multiple_of(at + cols - half, 8), half)
        G[w, :] = G[w, :] + qrd[r * half:(r + 1) * half]
    for r in range(rows):
        at = 16 + pitch * (r + radius)
        gl_ref[r * cols:(r + 1) * cols, :] = G[at:at + cols, :].astype(bf16)

    for c in st3:
        c.wait()
    if scatter:
        o3 = pl.multiple_of(o2 + lon * n3, 16)
        v = GF[pl.ds(o3, n3), :]
        for d in range(1, L):
            v = v + R3[d - 1].astype(f32)
        GA[pl.ds(o3, n3), :] = v.astype(bf16)
        cs = []
        for d in range(1, L):
            c = rcopy(GA.at[pl.ds(o3, n3)], GA.at[pl.ds(o3, n3)], a3s.at[d - 1], a3r.at[d - 1], {"lon": lax.rem(lon + d, L)})
            c.start()
            cs.append(c)
        for c in cs:
            c.wait()
    else:
        R3[lon] = GB[pl.ds(o2, n2), :]
        v = R3[0].astype(f32)
        for q in range(1, L):
            v = v + R3[q].astype(f32)
        GA[pl.ds(o2, n2), :] = v.astype(bf16)
    cs = []
    for d in range(1, M):
        c = rcopy(GA.at[pl.ds(o2, n2)], GA.at[pl.ds(o2, n2)], a2s.at[d - 1], a2r.at[d - 1], {"member": lax.rem(mem + d, M)})
        c.start()
        cs.append(c)
    for c in cs:
        c.wait()
    c = rcopy(GA.at[pl.ds(o1, n1)], GA.at[pl.ds(o1, n1)], a1s, a1r, {"lat": other})
    c.start()
    c.wait()
    gc_ref[:, :hc] = GA[0:KC, :].astype(f32) * scale
    gc_ref[:, hc:] = GA[KC:2 * KC, :].astype(f32) * scale
    go_ref[...] = GA[2 * KC:total, :fields].astype(f32) * scale


def local(mesh_shape, latent, target, quadrature, widths, conv_weight, output_weight):
    rows, cols, C = latent.shape[1:]
    K, _, taps_lat, taps_lon = quadrature.shape
    half = taps_lon // 2
    fields = output_weight.shape[1]
    L, M = mesh_shape["lon"], mesh_shape["member"]
    lats = mesh_shape["lat"]
    assert lats == 2
    pitch, slots, window, span = dims_of(rows, cols, taps_lat, half)
    n = rows * cols
    radius = taps_lat // 2
    hh = radius * half
    start = lax.axis_index("lat") * rows
    quad = lax.dynamic_slice_in_dim(quadrature, start, rows, 1)
    wid = lax.dynamic_slice_in_dim(widths, start, rows, 0)
    keep = jnp.abs(jnp.arange(taps_lon) - half)[None, :] <= wid[:, None]
    psi = jnp.where(keep[None, :, None, :], quad, jnp.zeros_like(quad)).astype(f32)
    base = jnp.pad(psi, ((0, 8 - K), (0, 0), (0, 0), (0, pitch - taps_lon))).transpose(1, 0, 2, 3)
    base = base.reshape(rows * 8, taps_lat * pitch)
    lead = 16 - half
    base = jnp.pad(base, ((0, 0), (lead, window - lead - taps_lat * pitch)))
    scale = 1.0 / math.sqrt(M * rows * lats * cols * L)
    sizes = (rows, cols, C, K, taps_lat, half, L, M, fields, scale)
    total = 2 * K * C + C
    n1 = total // 2
    n2 = n1 // M
    scatter = n2 % (16 * L) == 0
    r3 = (L - 1, n2 // L, 128) if scatter else (L, n2, 128)
    V = pltpu.VMEM
    D = pltpu.SemaphoreType.DMA
    scratch = [
        V((rows, K * cols, window), bf16), V((span, C), bf16), V((span, C), f32),
        V((n, K * C), bf16), V((n, K * C), bf16), V((n, C), f32), V((n, C), bf16),
        V((n, 128), bf16), V((M - 1, n, 128), bf16), V((C, 128), bf16), V((n, 128), bf16), V((n, C), bf16),
        V((total, 128), f32), V((total, 128), bf16), V((total, 128), bf16),
        V((rows * half, C), bf16), V((rows * half, C), bf16),
        V((slots * half, C), bf16), V((slots * half, C), bf16), V((radius * cols, C), bf16),
        V((slots * half, C), bf16), V((slots * half, C), bf16), V((radius * cols, C), bf16),
        V((rows * half, C), bf16), V((rows * half, C), bf16), V((radius * cols, C), bf16),
        V((hh, C), bf16), V((hh, C), bf16),
        V((n1, 128), bf16), V((M - 1, n2, 128), bf16), V(r3, bf16),
        D((5,)), D((5,)), D((M - 1, CHUNKS)), D((M - 1, CHUNKS)), D((5,)), D((5,)),
        D(()), D(()), D((M - 1,)), D((M - 1,)), D((L - 1,)), D((L - 1,)),
        D((L - 1,)), D((L - 1,)), D((M - 1,)), D((M - 1,)), D(()), D(()),
    ]
    spec = pl.BlockSpec(memory_space=pltpu.VMEM)
    gl, gc, go = pl.pallas_call(
        functools.partial(kernel, sizes),
        out_shape=(jax.ShapeDtypeStruct((n, C), bf16), jax.ShapeDtypeStruct((K * C, C), f32),
                   jax.ShapeDtypeStruct((C, fields), f32)),
        in_specs=[spec] * 5,
        out_specs=(spec,) * 3,
        scratch_shapes=scratch,
        compiler_params=pltpu.CompilerParams(
            collective_id=0, has_side_effects=True, vmem_limit_bytes=48 * 1024 * 1024),
    )(latent.reshape(n, C), target.reshape(n, fields), base, conv_weight, output_weight)
    return gl.reshape(1, rows, cols, C), gc, go


def solution(mesh):
    in_specs = (
        P(("groups", "member"), "lat", "lon", None),
        P(("groups", "lat"), "lon", None),
        P(),
        P(),
        P(),
        P(),
    )
    out_specs = (P(("groups", "member"), "lat", "lon", None), P("groups", None), P("groups", None))
    body = functools.partial(local, dict(mesh.shape))
    return jax.shard_map(body, mesh=mesh, in_specs=in_specs, out_specs=out_specs, check_vma=False)
```

```python
import functools
import math

import jax
import jax.numpy as jnp
from jax import lax
from jax.experimental import pallas as pl
from jax.experimental.pallas import tpu as pltpu
from jax.sharding import PartitionSpec as P

smoothing = 0.1
MESH = pl.DeviceIdType.MESH
f32 = jnp.float32
bf16 = jnp.bfloat16
CHUNKS = 4
PIECES = 3


def slope(d):
    return d * lax.rsqrt(d * d + smoothing * smoothing)


def dims_of(rows, cols, taps_lat, half):
    pitch = cols + 2 * half
    slots = rows + taps_lat - 1
    window = -(-(16 + taps_lat * pitch) // 128) * 128
    return pitch, slots, window, (rows - 1) * pitch + window


def kernel(sizes, wid_ref, lat_ref, tgt_ref, q_ref, cw_ref, ow_ref, gl_ref, gc_ref, go_ref,
           base, FP, T, X, G, basis, BG, DG, mixed, F, FR, wo, pg, hg, GF, GB, GA,
           SL, SR, RL, RR, RC, SL2, SR2, SC2, QL, QR, QC, QLd, QRd, R1, R2, R3,
           hs, hr, fs, fr, as_, ar, s1s, s1r, s2s, s2r, s3s, s3r, a3s, a3r, a2s, a2r, a1s, a1r):
    rows, cols, C, K, taps_lat, half, L, M, fields, scale = sizes
    radius = taps_lat // 2
    pitch, slots, window, span = dims_of(rows, cols, taps_lat, half)
    n = rows * cols
    per = rows // CHUNKS
    cn = per * cols
    lat = lax.axis_index("lat")
    lon = lax.axis_index("lon")
    mem = lax.axis_index("member")
    other = 1 - lat
    right = lax.rem(lon + 1, L)
    left = lax.rem(lon + L - 1, L)
    hh = radius * half

    def rcopy(src, dst, ss, rs, dev):
        return pltpu.make_async_remote_copy(
            src_ref=src, dst_ref=dst, send_sem=ss, recv_sem=rs, device_id=dev, device_id_type=MESH)

    barrier = pltpu.get_barrier_semaphore()
    peers = [{"lat": other}, {"lat": other, "lon": left}, {"lat": other, "lon": right}]
    peers += [{"lon": lax.rem(lon + d, L)} for d in range(1, L)]
    peers += [{"member": lax.rem(mem + d, M)} for d in range(1, M)]
    for dev in peers:
        pl.semaphore_signal(barrier, inc=1, device_id=dev, device_id_type=MESH)

    lat3 = lat_ref[...].astype(f32).reshape(rows, cols, C)
    SL[...] = lat3[:, :half].reshape(rows * half, C).astype(bf16)
    SR[...] = lat3[:, cols - half:].reshape(rows * half, C).astype(bf16)
    zero_halo = jnp.zeros((hh, C), bf16)
    edge = pl.multiple_of(lat * (hh + rows * half), 16)
    RL[pl.ds(edge, hh), :] = zero_halo
    RR[pl.ds(edge, hh), :] = zero_halo
    pl.semaphore_wait(barrier, len(peers))

    near = pl.multiple_of(other * (rows - radius) * half, 16)
    far = pl.multiple_of(lat * 0 + (1 - other) * (hh + rows * half), 16)
    nearrow = pl.multiple_of(other * (rows - radius) * cols, 16)
    inner = pl.ds(hh, rows * half)
    halo = [
        rcopy(SL, RR.at[inner], hs.at[0], hr.at[0], {"lon": left}),
        rcopy(SR, RL.at[inner], hs.at[1], hr.at[1], {"lon": right}),
        rcopy(SL.at[pl.ds(near, hh)], RR.at[pl.ds(far, hh)], hs.at[2], hr.at[2], {"lat": other, "lon": left}),
        rcopy(SR.at[pl.ds(near, hh)], RL.at[pl.ds(far, hh)], hs.at[3], hr.at[3], {"lat": other, "lon": right}),
        rcopy(lat_ref.at[pl.ds(nearrow, radius * cols)], RC, hs.at[4], hr.at[4], {"lat": other}),
    ]
    for c in halo:
        c.start()

    taps = q_ref.shape[0]
    taps_lon = taps // taps_lat
    nlat = 2 * rows
    tap = lax.broadcasted_iota(jnp.int32, (taps, window), 0)
    lane = lax.broadcasted_iota(jnp.int32, (taps, window), 1) - (16 - half)
    tap_a = tap // taps_lon
    place = (lane == tap_a * pitch + (tap - tap_a * taps_lon)).astype(bf16)
    base[...] = lax.dot_general(q_ref[...], place, (((0,), (0,)), ((), ())), preferred_element_type=f32)
    lane1 = lax.broadcasted_iota(jnp.int32, (1, window), 1) - (16 - half)
    offset = jnp.abs(lane1 - lane1 // pitch * pitch - half)

    def build(i, carry):
        row = lat * rows + i
        keep = offset <= wid_ref[row]
        for k in range(K):
            line = jnp.where(keep, base[pl.ds(k * nlat + row, 1), :], 0.0)
            line = jnp.broadcast_to(line, (cols, window))
            T[i, k * cols:(k + 1) * cols, :] = pltpu.roll(line, 0, 1, stride=1, stride_axis=0).astype(bf16)
        return carry
    lax.fori_loop(0, rows, build, 0)

    G[...] = jnp.zeros(G.shape, f32)
    wo[...] = jnp.concatenate([ow_ref[...].astype(f32), jnp.zeros((128 - fields, C), f32)], axis=0).astype(bf16)
    pg[...] = jnp.zeros(pg.shape, bf16)
    X[pl.ds(16 + slots * pitch, span - 16 - slots * pitch), :] = jnp.zeros((span - 16 - slots * pitch, C), bf16)
    for r in range(rows):
        X[16 + pitch * (r + radius):16 + pitch * (r + radius) + cols, :] = lat_ref[r * cols:(r + 1) * cols, :]
    zrow = jnp.zeros((cols, C), bf16)
    for r in range(radius):
        X[pl.ds(pl.multiple_of(16 + pitch * (r + lat * (rows + radius)), 16), cols), :] = zrow
    for c in halo:
        c.wait()
    for r in range(radius):
        X[pl.ds(pl.multiple_of(16 + pitch * (r + other * (rows + radius)), 16), cols), :] = RC[r * cols:(r + 1) * cols, :]
    rl = RL[...].astype(f32)
    rr = RR[...].astype(f32)
    z8 = jnp.zeros((half, C), f32)
    X[0:16, :] = jnp.concatenate([z8, rl[0:half]], axis=0).astype(bf16)
    for r in range(slots):
        nxt = rl[(r + 1) * half:(r + 2) * half] if r + 1 < slots else z8
        X[16 + pitch * r + cols:16 + pitch * (r + 1), :] = jnp.concatenate(
            [rr[r * half:(r + 1) * half], nxt], axis=0).astype(bf16)

    c0 = math.sqrt(2 / math.pi)
    groups = cn // 16
    lw = fields - 64
    assert groups * lw == 128
    pn = cn // 2 + 16
    fcopies = []
    for ch in range(CHUNKS):
        def conv(ii, carry, ch=ch):
            i = ch * per + ii
            out = jnp.dot(T[i], X[pl.ds(pl.multiple_of(i * pitch, 16), window), :], preferred_element_type=f32).astype(bf16)
            for k in range(K):
                basis[pl.ds(pl.multiple_of(i * cols, 16), cols), k * C:(k + 1) * C] = out[k * cols:(k + 1) * cols]
            return carry
        lax.fori_loop(0, per, conv, 0, unroll=True)
        sl = slice(ch * cn, (ch + 1) * cn)
        h = jnp.dot(basis[sl, :], cw_ref[...], preferred_element_type=f32)
        t = jnp.tanh(c0 * (h + 0.044715 * h * h * h))
        DG[sl, :] = 0.5 * (1 + t) + 0.5 * h * (1 - t * t) * (c0 * (1 + 3 * 0.044715 * h * h))
        mx = (lat_ref[sl, :].astype(f32) + 0.5 * h * (1 + t)).astype(bf16)
        mixed[sl, :] = mx
        fc = lax.dot_general(mx, wo[...], (((1,), (1,)), ((), ())), preferred_element_type=f32)
        F[sl, :] = fc.astype(bf16)
        psl = pl.ds(ch * pn, pn)
        both = jnp.concatenate([fc[:cn // 2, :64], fc[cn // 2:, :64]], axis=1)
        rest = jnp.concatenate([fc[g * 16:(g + 1) * 16, 64:fields] for g in range(groups)], axis=1)
        FP[ch * pn:(ch + 1) * pn, :] = jnp.concatenate([both, rest], axis=0).astype(bf16)
        cs = []
        for d in range(1, M):
            c = rcopy(FP.at[psl], FR.at[d - 1, psl], fs.at[d - 1, ch], fr.at[d - 1, ch],
                      {"member": lax.rem(mem + d, M)})
            c.start()
            cs.append(c)
        fcopies.append(cs)

    for ch in range(CHUNKS):
        sl = slice(ch * cn, (ch + 1) * cn)
        mine = F[sl, :fields].astype(f32)
        first = slope(mine - tgt_ref[sl, :])
        for c in fcopies[ch]:
            c.wait()
        pair = jnp.zeros_like(mine)
        for d in range(1, M):
            got = FR[d - 1, ch * pn:(ch + 1) * pn, :].astype(f32)
            body = got[:cn // 2]
            rest = got[cn // 2:]
            theirs = jnp.concatenate([
                jnp.concatenate([body[:, :64], body[:, 64:]], axis=0),
                jnp.concatenate([rest[:, g * lw:(g + 1) * lw] for g in range(groups)], axis=0)], axis=1)
            pair = pair + slope(mine - theirs)
        pg[sl, :fields] = (first - pair * (1.0 / (M - 1))).astype(bf16)
        up = jnp.dot(pg[sl, :], wo[...], preferred_element_type=f32)
        for ii in range(per):
            r = ch * per + ii + radius
            G[16 + pitch * r:16 + pitch * r + cols, :] = up[ii * cols:(ii + 1) * cols]
        hg[sl, :] = (up * DG[sl, :]).astype(bf16)

    KC = K * C
    hc = C // 2
    total = 2 * KC + 256
    tc = total // PIECES
    n1 = tc // 2
    n2 = n1 // M
    scatter = n2 % (16 * L) == 0
    n3 = n2 // L if scatter else n2
    o1 = [pl.multiple_of(c * tc + lat * n1, 16) for c in range(PIECES)]
    o1o = [pl.multiple_of(c * tc + other * n1, 16) for c in range(PIECES)]
    o2 = [pl.multiple_of(o1[c] + mem * n2, 16) for c in range(PIECES)]
    tn = (((0,), (0,)), ((), ()))
    st1 = []

    def ready(done):
        while len(st1) < PIECES and (len(st1) + 1) * tc <= done:
            c = len(st1)
            copy = rcopy(GB.at[pl.ds(o1o[c], n1)], R1.at[c], s1s.at[c], s1r.at[c], {"lat": other})
            copy.start()
            st1.append(copy)

    hgv = hg[...]
    for k in range(K):
        g = lax.dot_general(basis[:, k * C:(k + 1) * C], hgv, tn, preferred_element_type=f32)
        for half_id in range(2):
            part = g[:, half_id * hc:(half_id + 1) * hc]
            at = (2 * k + half_id) * C
            GF[at:at + C, :] = part
            GB[at:at + C, :] = part.astype(bf16)
        ready(2 * (k + 1) * C)
    g = lax.dot_general(pg[...], mixed[...], tn, preferred_element_type=f32)
    for half_id in range(2):
        part = g[:, half_id * hc:(half_id + 1) * hc]
        at = 2 * KC + half_id * 128
        GF[at:at + 128, :] = part
        GB[at:at + 128, :] = part.astype(bf16)
    ready(total)

    def adjoint(first_row, last_row):
        lo, size = first_row * cols, (last_row - first_row) * cols
        BG[lo:lo + size, :] = lax.dot_general(
            hg[lo:lo + size, :], cw_ref[...], (((1,), (1,)), ((), ())), preferred_element_type=f32).astype(bf16)

        def body(i, carry):
            at = pl.ds(pl.multiple_of(i * cols, 16), cols)
            stacked = jnp.concatenate([BG[at, k * C:(k + 1) * C] for k in range(K)], axis=0)
            out = lax.dot_general(T[i], stacked, tn, preferred_element_type=f32)
            w = pl.ds(pl.multiple_of(i * pitch, 16), window)
            G[w, :] = G[w, :] + out
            return carry
        lax.fori_loop(first_row, last_row, body, 0)

    quarter = rows // 4
    adjoint(0, quarter)
    st2 = []
    for c in range(PIECES):
        st1[c].wait()
        w = pl.ds(o1[c], n1)
        v = GF[w, :] + R1[c].astype(f32)
        GF[w, :] = v
        GB[w, :] = v.astype(bf16)
        cs = []
        for d in range(1, M):
            q = lax.rem(mem + d, M)
            copy = rcopy(GB.at[pl.ds(pl.multiple_of(o1[c] + q * n2, 16), n2)], R2.at[c, d - 1],
                         s2s.at[c, d - 1], s2r.at[c, d - 1], {"member": q})
            copy.start()
            cs.append(copy)
        st2.append(cs)

    st3 = []
    for c in range(PIECES):
        adjoint((c + 1) * quarter, (c + 2) * quarter)
        for copy in st2[c]:
            copy.wait()
        w = pl.ds(o2[c], n2)
        v = GF[w, :]
        for d in range(1, M):
            v = v + R2[c, d - 1].astype(f32)
        GF[w, :] = v
        GB[w, :] = v.astype(bf16)
        cs = []
        for d in range(1, L):
            q = lax.rem(lon + d, L)
            src = GB.at[pl.ds(pl.multiple_of(o2[c] + q * n3, 16), n3)] if scatter else GB.at[w]
            dst = R3.at[c, d - 1] if scatter else R3.at[c, lon]
            copy = rcopy(src, dst, s3s.at[c, d - 1], s3r.at[c, d - 1], {"lon": q})
            copy.start()
            cs.append(copy)
        st3.append(cs)

    SR2[...] = jnp.concatenate([G[16 + pitch * r + cols:16 + pitch * r + cols + half, :] for r in range(slots)], axis=0).astype(bf16)
    SL2[...] = jnp.concatenate([G[16 + pitch * r - half:16 + pitch * r, :] for r in range(slots)], axis=0).astype(bf16)
    for r in range(radius):
        SC2[r * cols:(r + 1) * cols, :] = G[pl.ds(pl.multiple_of(16 + pitch * (r + other * (rows + radius)), 16), cols), :].astype(bf16)
    beyond = pl.multiple_of(other * (hh + rows * half), 16)
    back = [
        rcopy(SR2.at[inner], QL, as_.at[0], ar.at[0], {"lon": right}),
        rcopy(SL2.at[inner], QR, as_.at[1], ar.at[1], {"lon": left}),
        rcopy(SR2.at[pl.ds(beyond, hh)], QLd, as_.at[2], ar.at[2], {"lat": other, "lon": right}),
        rcopy(SL2.at[pl.ds(beyond, hh)], QRd, as_.at[3], ar.at[3], {"lat": other, "lon": left}),
        rcopy(SC2, QC, as_.at[4], ar.at[4], {"lat": other}),
    ]
    for c in back:
        c.start()

    ag3 = []
    for c in range(PIECES):
        for copy in st3[c]:
            copy.wait()
        cs = []
        if scatter:
            w = pl.ds(pl.multiple_of(o2[c] + lon * n3, 16), n3)
            v = GF[w, :]
            for d in range(1, L):
                v = v + R3[c, d - 1].astype(f32)
            GA[w, :] = v.astype(bf16)
            for d in range(1, L):
                copy = rcopy(GA.at[w], GA.at[w], a3s.at[c, d - 1], a3r.at[c, d - 1], {"lon": lax.rem(lon + d, L)})
                copy.start()
                cs.append(copy)
        else:
            w = pl.ds(o2[c], n2)
            R3[c, lon] = GB[w, :]
            v = R3[c, 0].astype(f32)
            for q in range(1, L):
                v = v + R3[c, q].astype(f32)
            GA[w, :] = v.astype(bf16)
        ag3.append(cs)

    for c in back:
        c.wait()
    ql = QL[...].astype(f32)
    qr = QR[...].astype(f32)
    qld = QLd[...].astype(f32)
    qrd = QRd[...].astype(f32)
    for r in range(rows):
        at = 16 + pitch * (r + radius)
        G[at:at + half, :] = G[at:at + half, :] + ql[r * half:(r + 1) * half]
        G[at + cols - half:at + cols, :] = G[at + cols - half:at + cols, :] + qr[r * half:(r + 1) * half]
    for r in range(radius):
        at = 16 + pitch * (radius + r + other * (rows - radius))
        w = pl.ds(pl.multiple_of(at, 16), cols)
        G[w, :] = G[w, :] + QC[r * cols:(r + 1) * cols, :].astype(f32)
        w = pl.ds(pl.multiple_of(at, 8), half)
        G[w, :] = G[w, :] + qld[r * half:(r + 1) * half]
        w = pl.ds(pl.multiple_of(at + cols - half, 8), half)
        G[w, :] = G[w, :] + qrd[r * half:(r + 1) * half]
    ag2 = []
    for c in range(PIECES):
        for copy in ag3[c]:
            copy.wait()
        w = pl.ds(o2[c], n2)
        cs = []
        for d in range(1, M):
            copy = rcopy(GA.at[w], GA.at[w], a2s.at[c, d - 1], a2r.at[c, d - 1], {"member": lax.rem(mem + d, M)})
            copy.start()
            cs.append(copy)
        ag2.append(cs)
    for r in range(rows):
        at = 16 + pitch * (r + radius)
        gl_ref[r * cols:(r + 1) * cols, :] = G[at:at + cols, :].astype(bf16)

    ag1 = []
    for c in range(PIECES):
        for copy in ag2[c]:
            copy.wait()
        w = pl.ds(o1[c], n1)
        copy = rcopy(GA.at[w], GA.at[w], a1s.at[c], a1r.at[c], {"lat": other})
        copy.start()
        ag1.append(copy)
    block = 0
    for c in range(PIECES):
        ag1[c].wait()
        while block < 2 * K and (block + 1) * C <= (c + 1) * tc:
            k, half_id = block // 2, block % 2
            gc_ref[k * C:(k + 1) * C, half_id * hc:(half_id + 1) * hc] = GA[block * C:(block + 1) * C, :].astype(f32) * scale
            block += 1
    for half_id in range(2):
        at = 2 * KC + half_id * 128
        go_ref[:, half_id * hc:(half_id + 1) * hc] = GA[at:at + 128, :].astype(f32)[:fields] * scale


def local(mesh_shape, latent, target, quadrature, widths, conv_weight, output_weight):
    rows, cols, C = latent.shape[1:]
    K, _, taps_lat, taps_lon = quadrature.shape
    half = taps_lon // 2
    fields = output_weight.shape[1]
    L, M = mesh_shape["lon"], mesh_shape["member"]
    lats = mesh_shape["lat"]
    assert lats == 2
    pitch, slots, window, span = dims_of(rows, cols, taps_lat, half)
    n = rows * cols
    radius = taps_lat // 2
    hh = radius * half
    q2 = quadrature.transpose(2, 3, 0, 1).reshape(taps_lat * taps_lon, K * rows * lats)
    scale = 1.0 / math.sqrt(M * rows * lats * cols * L)
    sizes = (rows, cols, C, K, taps_lat, half, L, M, fields, scale)
    total = 2 * K * C + 256
    n1 = total // PIECES // 2
    n2 = n1 // M
    scatter = n2 % (16 * L) == 0
    r3 = (PIECES, L - 1, n2 // L, 128) if scatter else (PIECES, L, n2, 128)
    pn = n // CHUNKS // 2 + 16
    V = pltpu.VMEM
    D = pltpu.SemaphoreType.DMA
    scratch = [
        V((K * rows * lats, window), f32), V((CHUNKS * pn, 128), bf16),
        V((rows, K * cols, window), bf16), V((span, C), bf16), V((span, C), f32),
        V((n, K * C), bf16), V((n, K * C), bf16), V((n, C), f32), V((n, C), bf16),
        V((n, 128), bf16), V((M - 1, CHUNKS * pn, 128), bf16), V((128, C), bf16), V((n, 128), bf16), V((n, C), bf16),
        V((total, 128), f32), V((total, 128), bf16), V((total, 128), bf16),
        V((rows * half, C), bf16), V((rows * half, C), bf16),
        V((slots * half, C), bf16), V((slots * half, C), bf16), V((radius * cols, C), bf16),
        V((slots * half, C), bf16), V((slots * half, C), bf16), V((radius * cols, C), bf16),
        V((rows * half, C), bf16), V((rows * half, C), bf16), V((radius * cols, C), bf16),
        V((hh, C), bf16), V((hh, C), bf16),
        V((PIECES, n1, 128), bf16), V((PIECES, M - 1, n2, 128), bf16), V(r3, bf16),
        D((5,)), D((5,)), D((M - 1, CHUNKS)), D((M - 1, CHUNKS)), D((5,)), D((5,)),
        D((PIECES,)), D((PIECES,)), D((PIECES, M - 1)), D((PIECES, M - 1)), D((PIECES, L - 1)), D((PIECES, L - 1)),
        D((PIECES, L - 1)), D((PIECES, L - 1)), D((PIECES, M - 1)), D((PIECES, M - 1)), D((PIECES,)), D((PIECES,)),
    ]
    spec = pl.BlockSpec(memory_space=pltpu.VMEM)
    gl, gc, go = pl.pallas_call(
        functools.partial(kernel, sizes),
        out_shape=(jax.ShapeDtypeStruct((n, C), bf16), jax.ShapeDtypeStruct((K * C, C), f32),
                   jax.ShapeDtypeStruct((fields, C), f32)),
        in_specs=[pl.BlockSpec(memory_space=pltpu.SMEM)] + [spec] * 5,
        out_specs=(spec,) * 3,
        scratch_shapes=scratch,
        compiler_params=pltpu.CompilerParams(
            collective_id=0, has_side_effects=True, vmem_limit_bytes=48 * 1024 * 1024),
    )(widths, latent.reshape(n, C), target.reshape(n, fields), q2, conv_weight, output_weight.T)
    return gl.reshape(1, rows, cols, C), gc, go.T


def solution(mesh):
    in_specs = (
        P(("groups", "member"), "lat", "lon", None),
        P(("groups", "lat"), "lon", None),
        P(),
        P(),
        P(),
        P(),
    )
    out_specs = (P(("groups", "member"), "lat", "lon", None), P("groups", None), P("groups", None))
    body = functools.partial(local, dict(mesh.shape))
    return jax.shard_map(body, mesh=mesh, in_specs=in_specs, out_specs=out_specs, check_vma=False)
```

```python
import functools
import math

import jax
import jax.numpy as jnp
from jax import lax
from jax.experimental import pallas as pl
from jax.experimental.pallas import tpu as pltpu
from jax.sharding import PartitionSpec as P

smoothing = 0.1
MESH = pl.DeviceIdType.MESH
f32 = jnp.float32
bf16 = jnp.bfloat16
CHUNKS = 4
PIECES = 3


def slope(d):
    return d * lax.rsqrt(d * d + smoothing * smoothing)


def dims_of(rows, cols, taps_lat, half):
    pitch = cols + 2 * half
    slots = rows + taps_lat - 1
    window = -(-(16 + taps_lat * pitch) // 128) * 128
    return pitch, slots, window, (rows - 1) * pitch + window


def kernel(sizes, wid_ref, lat_hbm, tgt_hbm, q_ref, cw_hbm, ow_ref, gl_ref, gc_ref, go_ref,
           lat_ref, tgt_ref, cw_ref, ins, base, FP, T, X, G, basis, BG, DG, mixed, F, FR, wo, pg, hg, GF, GB, GA,
           SL, SR, RL, RR, RC, SL2, SR2, SC2, QL, QR, QC, QLd, QRd, R1, R2, R3,
           hs, hr, fs, fr, as_, ar, s1s, s1r, s2s, s2r, s3s, s3r, a3s, a3r, a2s, a2r, a1s, a1r):
    rows, cols, C, K, taps_lat, half, L, M, fields, scale = sizes
    radius = taps_lat // 2
    pitch, slots, window, span = dims_of(rows, cols, taps_lat, half)
    n = rows * cols
    per = rows // CHUNKS
    cn = per * cols
    lat = lax.axis_index("lat")
    lon = lax.axis_index("lon")
    mem = lax.axis_index("member")
    other = 1 - lat
    right = lax.rem(lon + 1, L)
    left = lax.rem(lon + L - 1, L)
    hh = radius * half

    def rcopy(src, dst, ss, rs, dev):
        return pltpu.make_async_remote_copy(
            src_ref=src, dst_ref=dst, send_sem=ss, recv_sem=rs, device_id=dev, device_id_type=MESH)

    loads = [pltpu.make_async_copy(src, dst, ins.at[i]) for i, (src, dst) in enumerate(
        [(lat_hbm, lat_ref), (cw_hbm, cw_ref), (tgt_hbm, tgt_ref)])]
    for c in loads:
        c.start()
    barrier = pltpu.get_barrier_semaphore()
    peers = [{"lat": other}, {"lat": other, "lon": left}, {"lat": other, "lon": right}]
    peers += [{"lon": lax.rem(lon + d, L)} for d in range(1, L)]
    peers += [{"member": lax.rem(mem + d, M)} for d in range(1, M)]
    for dev in peers:
        pl.semaphore_signal(barrier, inc=1, device_id=dev, device_id_type=MESH)

    loads[0].wait()
    lat3 = lat_ref[...].astype(f32).reshape(rows, cols, C)
    SL[...] = lat3[:, :half].reshape(rows * half, C).astype(bf16)
    SR[...] = lat3[:, cols - half:].reshape(rows * half, C).astype(bf16)
    zero_halo = jnp.zeros((hh, C), bf16)
    edge = pl.multiple_of(lat * (hh + rows * half), 16)
    RL[pl.ds(edge, hh), :] = zero_halo
    RR[pl.ds(edge, hh), :] = zero_halo
    pl.semaphore_wait(barrier, len(peers))

    near = pl.multiple_of(other * (rows - radius) * half, 16)
    far = pl.multiple_of(lat * 0 + (1 - other) * (hh + rows * half), 16)
    nearrow = pl.multiple_of(other * (rows - radius) * cols, 16)
    inner = pl.ds(hh, rows * half)
    halo = [
        rcopy(SL, RR.at[inner], hs.at[0], hr.at[0], {"lon": left}),
        rcopy(SR, RL.at[inner], hs.at[1], hr.at[1], {"lon": right}),
        rcopy(SL.at[pl.ds(near, hh)], RR.at[pl.ds(far, hh)], hs.at[2], hr.at[2], {"lat": other, "lon": left}),
        rcopy(SR.at[pl.ds(near, hh)], RL.at[pl.ds(far, hh)], hs.at[3], hr.at[3], {"lat": other, "lon": right}),
        rcopy(lat_ref.at[pl.ds(nearrow, radius * cols)], RC, hs.at[4], hr.at[4], {"lat": other}),
    ]
    for c in halo:
        c.start()

    taps = q_ref.shape[0]
    taps_lon = taps // taps_lat
    nlat = 2 * rows
    tap = lax.broadcasted_iota(jnp.int32, (taps, window), 0)
    lane = lax.broadcasted_iota(jnp.int32, (taps, window), 1) - (16 - half)
    tap_a = tap // taps_lon
    place = (lane == tap_a * pitch + (tap - tap_a * taps_lon)).astype(bf16)
    base[...] = lax.dot_general(q_ref[...], place, (((0,), (0,)), ((), ())), preferred_element_type=f32)
    lane1 = lax.broadcasted_iota(jnp.int32, (1, window), 1) - (16 - half)
    offset = jnp.abs(lane1 - lane1 // pitch * pitch - half)

    def build(i, carry):
        row = lat * rows + i
        keep = offset <= wid_ref[row]
        for k in range(K):
            line = jnp.where(keep, base[pl.ds(k * nlat + row, 1), :], 0.0)
            line = jnp.broadcast_to(line, (cols, window))
            T[i, k * cols:(k + 1) * cols, :] = pltpu.roll(line, 0, 1, stride=1, stride_axis=0).astype(bf16)
        return carry
    lax.fori_loop(0, rows, build, 0)

    G[...] = jnp.zeros(G.shape, f32)
    wo[...] = jnp.concatenate([ow_ref[...].astype(f32), jnp.zeros((128 - fields, C), f32)], axis=0).astype(bf16)
    pg[...] = jnp.zeros(pg.shape, bf16)
    X[pl.ds(16 + slots * pitch, span - 16 - slots * pitch), :] = jnp.zeros((span - 16 - slots * pitch, C), bf16)
    for r in range(rows):
        X[16 + pitch * (r + radius):16 + pitch * (r + radius) + cols, :] = lat_ref[r * cols:(r + 1) * cols, :]
    zrow = jnp.zeros((cols, C), bf16)
    for r in range(radius):
        X[pl.ds(pl.multiple_of(16 + pitch * (r + lat * (rows + radius)), 16), cols), :] = zrow
    for c in halo:
        c.wait()
    for r in range(radius):
        X[pl.ds(pl.multiple_of(16 + pitch * (r + other * (rows + radius)), 16), cols), :] = RC[r * cols:(r + 1) * cols, :]
    rl = RL[...].astype(f32)
    rr = RR[...].astype(f32)
    z8 = jnp.zeros((half, C), f32)
    X[0:16, :] = jnp.concatenate([z8, rl[0:half]], axis=0).astype(bf16)
    for r in range(slots):
        nxt = rl[(r + 1) * half:(r + 2) * half] if r + 1 < slots else z8
        X[16 + pitch * r + cols:16 + pitch * (r + 1), :] = jnp.concatenate(
            [rr[r * half:(r + 1) * half], nxt], axis=0).astype(bf16)

    loads[1].wait()
    loads[2].wait()
    c0 = math.sqrt(2 / math.pi)
    groups = cn // 16
    lw = fields - 64
    assert groups * lw == 128
    pn = cn // 2 + 16
    fcopies = []
    for ch in range(CHUNKS):
        def conv(ii, carry, ch=ch):
            i = ch * per + ii
            out = jnp.dot(T[i], X[pl.ds(pl.multiple_of(i * pitch, 16), window), :], preferred_element_type=f32).astype(bf16)
            for k in range(K):
                basis[pl.ds(pl.multiple_of(i * cols, 16), cols), k * C:(k + 1) * C] = out[k * cols:(k + 1) * cols]
            return carry
        lax.fori_loop(0, per, conv, 0, unroll=True)
        sl = slice(ch * cn, (ch + 1) * cn)
        h = jnp.dot(basis[sl, :], cw_ref[...], preferred_element_type=f32)
        t = jnp.tanh(c0 * (h + 0.044715 * h * h * h))
        DG[sl, :] = 0.5 * (1 + t) + 0.5 * h * (1 - t * t) * (c0 * (1 + 3 * 0.044715 * h * h))
        mx = (lat_ref[sl, :].astype(f32) + 0.5 * h * (1 + t)).astype(bf16)
        mixed[sl, :] = mx
        fc = lax.dot_general(mx, wo[...], (((1,), (1,)), ((), ())), preferred_element_type=f32)
        F[sl, :] = fc.astype(bf16)
        psl = pl.ds(ch * pn, pn)
        both = jnp.concatenate([fc[:cn // 2, :64], fc[cn // 2:, :64]], axis=1)
        rest = jnp.concatenate([fc[g * 16:(g + 1) * 16, 64:fields] for g in range(groups)], axis=1)
        FP[ch * pn:(ch + 1) * pn, :] = jnp.concatenate([both, rest], axis=0).astype(bf16)
        cs = []
        for d in range(1, M):
            c = rcopy(FP.at[psl], FR.at[d - 1, psl], fs.at[d - 1, ch], fr.at[d - 1, ch],
                      {"member": lax.rem(mem + d, M)})
            c.start()
            cs.append(c)
        fcopies.append(cs)

    for ch in range(CHUNKS):
        sl = slice(ch * cn, (ch + 1) * cn)
        mine = F[sl, :fields].astype(f32)
        first = slope(mine - tgt_ref[sl, :])
        for c in fcopies[ch]:
            c.wait()
        pair = jnp.zeros_like(mine)
        for d in range(1, M):
            got = FR[d - 1, ch * pn:(ch + 1) * pn, :].astype(f32)
            body = got[:cn // 2]
            rest = got[cn // 2:]
            theirs = jnp.concatenate([
                jnp.concatenate([body[:, :64], body[:, 64:]], axis=0),
                jnp.concatenate([rest[:, g * lw:(g + 1) * lw] for g in range(groups)], axis=0)], axis=1)
            pair = pair + slope(mine - theirs)
        pg[sl, :fields] = (first - pair * (1.0 / (M - 1))).astype(bf16)
        up = jnp.dot(pg[sl, :], wo[...], preferred_element_type=f32)
        for ii in range(per):
            r = ch * per + ii + radius
            G[16 + pitch * r:16 + pitch * r + cols, :] = up[ii * cols:(ii + 1) * cols]
        hg[sl, :] = (up * DG[sl, :]).astype(bf16)

    KC = K * C
    hc = C // 2
    total = 2 * KC + 256
    tc = total // PIECES
    n1 = tc // 2
    n2 = n1 // M
    scatter = n2 % (16 * L) == 0
    n3 = n2 // L if scatter else n2
    o1 = [pl.multiple_of(c * tc + lat * n1, 16) for c in range(PIECES)]
    o1o = [pl.multiple_of(c * tc + other * n1, 16) for c in range(PIECES)]
    o2 = [pl.multiple_of(o1[c] + mem * n2, 16) for c in range(PIECES)]
    tn = (((0,), (0,)), ((), ()))
    st1 = []

    def ready(done):
        while len(st1) < PIECES and (len(st1) + 1) * tc <= done:
            c = len(st1)
            copy = rcopy(GB.at[pl.ds(o1o[c], n1)], R1.at[c], s1s.at[c], s1r.at[c], {"lat": other})
            copy.start()
            st1.append(copy)

    hgv = hg[...]
    for k in range(K):
        g = lax.dot_general(basis[:, k * C:(k + 1) * C], hgv, tn, preferred_element_type=f32)
        for half_id in range(2):
            part = g[:, half_id * hc:(half_id + 1) * hc]
            at = (2 * k + half_id) * C
            GF[at:at + C, :] = part
            GB[at:at + C, :] = part.astype(bf16)
        ready(2 * (k + 1) * C)
    g = lax.dot_general(pg[...], mixed[...], tn, preferred_element_type=f32)
    for half_id in range(2):
        part = g[:, half_id * hc:(half_id + 1) * hc]
        at = 2 * KC + half_id * 128
        GF[at:at + 128, :] = part
        GB[at:at + 128, :] = part.astype(bf16)
    ready(total)

    def adjoint(first_row, last_row):
        lo, size = first_row * cols, (last_row - first_row) * cols
        BG[lo:lo + size, :] = lax.dot_general(
            hg[lo:lo + size, :], cw_ref[...], (((1,), (1,)), ((), ())), preferred_element_type=f32).astype(bf16)

        def body(i, carry):
            at = pl.ds(pl.multiple_of(i * cols, 16), cols)
            stacked = jnp.concatenate([BG[at, k * C:(k + 1) * C] for k in range(K)], axis=0)
            out = lax.dot_general(T[i], stacked, tn, preferred_element_type=f32)
            w = pl.ds(pl.multiple_of(i * pitch, 16), window)
            G[w, :] = G[w, :] + out
            return carry
        lax.fori_loop(first_row, last_row, body, 0)

    quarter = rows // 4
    adjoint(0, quarter)
    st2 = []
    for c in range(PIECES):
        st1[c].wait()
        w = pl.ds(o1[c], n1)
        v = GF[w, :] + R1[c].astype(f32)
        GF[w, :] = v
        GB[w, :] = v.astype(bf16)
        cs = []
        for d in range(1, M):
            q = lax.rem(mem + d, M)
            copy = rcopy(GB.at[pl.ds(pl.multiple_of(o1[c] + q * n2, 16), n2)], R2.at[c, d - 1],
                         s2s.at[c, d - 1], s2r.at[c, d - 1], {"member": q})
            copy.start()
            cs.append(copy)
        st2.append(cs)

    st3 = []
    for c in range(PIECES):
        adjoint((c + 1) * quarter, (c + 2) * quarter)
        for copy in st2[c]:
            copy.wait()
        w = pl.ds(o2[c], n2)
        v = GF[w, :]
        for d in range(1, M):
            v = v + R2[c, d - 1].astype(f32)
        GF[w, :] = v
        GB[w, :] = v.astype(bf16)
        cs = []
        for d in range(1, L):
            q = lax.rem(lon + d, L)
            src = GB.at[pl.ds(pl.multiple_of(o2[c] + q * n3, 16), n3)] if scatter else GB.at[w]
            dst = R3.at[c, d - 1] if scatter else R3.at[c, lon]
            copy = rcopy(src, dst, s3s.at[c, d - 1], s3r.at[c, d - 1], {"lon": q})
            copy.start()
            cs.append(copy)
        st3.append(cs)

    SR2[...] = jnp.concatenate([G[16 + pitch * r + cols:16 + pitch * r + cols + half, :] for r in range(slots)], axis=0).astype(bf16)
    SL2[...] = jnp.concatenate([G[16 + pitch * r - half:16 + pitch * r, :] for r in range(slots)], axis=0).astype(bf16)
    for r in range(radius):
        SC2[r * cols:(r + 1) * cols, :] = G[pl.ds(pl.multiple_of(16 + pitch * (r + other * (rows + radius)), 16), cols), :].astype(bf16)
    beyond = pl.multiple_of(other * (hh + rows * half), 16)
    back = [
        rcopy(SR2.at[inner], QL, as_.at[0], ar.at[0], {"lon": right}),
        rcopy(SL2.at[inner], QR, as_.at[1], ar.at[1], {"lon": left}),
        rcopy(SR2.at[pl.ds(beyond, hh)], QLd, as_.at[2], ar.at[2], {"lat": other, "lon": right}),
        rcopy(SL2.at[pl.ds(beyond, hh)], QRd, as_.at[3], ar.at[3], {"lat": other, "lon": left}),
        rcopy(SC2, QC, as_.at[4], ar.at[4], {"lat": other}),
    ]
    for c in back:
        c.start()

    ag3 = []
    for c in range(PIECES):
        for copy in st3[c]:
            copy.wait()
        cs = []
        if scatter:
            w = pl.ds(pl.multiple_of(o2[c] + lon * n3, 16), n3)
            v = GF[w, :]
            for d in range(1, L):
                v = v + R3[c, d - 1].astype(f32)
            GA[w, :] = v.astype(bf16)
            for d in range(1, L):
                copy = rcopy(GA.at[w], GA.at[w], a3s.at[c, d - 1], a3r.at[c, d - 1], {"lon": lax.rem(lon + d, L)})
                copy.start()
                cs.append(copy)
        else:
            w = pl.ds(o2[c], n2)
            R3[c, lon] = GB[w, :]
            v = R3[c, 0].astype(f32)
            for q in range(1, L):
                v = v + R3[c, q].astype(f32)
            GA[w, :] = v.astype(bf16)
        ag3.append(cs)

    for c in back:
        c.wait()
    ql = QL[...].astype(f32)
    qr = QR[...].astype(f32)
    qld = QLd[...].astype(f32)
    qrd = QRd[...].astype(f32)
    for r in range(rows):
        at = 16 + pitch * (r + radius)
        G[at:at + half, :] = G[at:at + half, :] + ql[r * half:(r + 1) * half]
        G[at + cols - half:at + cols, :] = G[at + cols - half:at + cols, :] + qr[r * half:(r + 1) * half]
    for r in range(radius):
        at = 16 + pitch * (radius + r + other * (rows - radius))
        w = pl.ds(pl.multiple_of(at, 16), cols)
        G[w, :] = G[w, :] + QC[r * cols:(r + 1) * cols, :].astype(f32)
        w = pl.ds(pl.multiple_of(at, 8), half)
        G[w, :] = G[w, :] + qld[r * half:(r + 1) * half]
        w = pl.ds(pl.multiple_of(at + cols - half, 8), half)
        G[w, :] = G[w, :] + qrd[r * half:(r + 1) * half]
    ag2 = []
    for c in range(PIECES):
        for copy in ag3[c]:
            copy.wait()
        w = pl.ds(o2[c], n2)
        cs = []
        for d in range(1, M):
            copy = rcopy(GA.at[w], GA.at[w], a2s.at[c, d - 1], a2r.at[c, d - 1], {"member": lax.rem(mem + d, M)})
            copy.start()
            cs.append(copy)
        ag2.append(cs)
    for r in range(rows):
        at = 16 + pitch * (r + radius)
        gl_ref[r * cols:(r + 1) * cols, :] = G[at:at + cols, :].astype(bf16)

    ag1 = []
    for c in range(PIECES):
        for copy in ag2[c]:
            copy.wait()
        w = pl.ds(o1[c], n1)
        copy = rcopy(GA.at[w], GA.at[w], a1s.at[c], a1r.at[c], {"lat": other})
        copy.start()
        ag1.append(copy)
    block = 0
    for c in range(PIECES):
        ag1[c].wait()
        while block < 2 * K and (block + 1) * C <= (c + 1) * tc:
            k, half_id = block // 2, block % 2
            gc_ref[k * C:(k + 1) * C, half_id * hc:(half_id + 1) * hc] = GA[block * C:(block + 1) * C, :].astype(f32) * scale
            block += 1
    for half_id in range(2):
        at = 2 * KC + half_id * 128
        go_ref[:, half_id * hc:(half_id + 1) * hc] = GA[at:at + 128, :].astype(f32)[:fields] * scale


def local(mesh_shape, latent, target, quadrature, widths, conv_weight, output_weight):
    rows, cols, C = latent.shape[1:]
    K, _, taps_lat, taps_lon = quadrature.shape
    half = taps_lon // 2
    fields = output_weight.shape[1]
    L, M = mesh_shape["lon"], mesh_shape["member"]
    lats = mesh_shape["lat"]
    assert lats == 2
    pitch, slots, window, span = dims_of(rows, cols, taps_lat, half)
    n = rows * cols
    radius = taps_lat // 2
    hh = radius * half
    q2 = quadrature.transpose(2, 3, 0, 1).reshape(taps_lat * taps_lon, K * rows * lats)
    scale = 1.0 / math.sqrt(M * rows * lats * cols * L)
    sizes = (rows, cols, C, K, taps_lat, half, L, M, fields, scale)
    total = 2 * K * C + 256
    n1 = total // PIECES // 2
    n2 = n1 // M
    scatter = n2 % (16 * L) == 0
    r3 = (PIECES, L - 1, n2 // L, 128) if scatter else (PIECES, L, n2, 128)
    pn = n // CHUNKS // 2 + 16
    V = pltpu.VMEM
    D = pltpu.SemaphoreType.DMA
    scratch = [
        V((n, C), bf16), V((n, fields), f32), V((K * C, C), bf16), D((3,)),
        V((K * rows * lats, window), f32), V((CHUNKS * pn, 128), bf16),
        V((rows, K * cols, window), bf16), V((span, C), bf16), V((span, C), f32),
        V((n, K * C), bf16), V((n, K * C), bf16), V((n, C), f32), V((n, C), bf16),
        V((n, 128), bf16), V((M - 1, CHUNKS * pn, 128), bf16), V((128, C), bf16), V((n, 128), bf16), V((n, C), bf16),
        V((total, 128), f32), V((total, 128), bf16), V((total, 128), bf16),
        V((rows * half, C), bf16), V((rows * half, C), bf16),
        V((slots * half, C), bf16), V((slots * half, C), bf16), V((radius * cols, C), bf16),
        V((slots * half, C), bf16), V((slots * half, C), bf16), V((radius * cols, C), bf16),
        V((rows * half, C), bf16), V((rows * half, C), bf16), V((radius * cols, C), bf16),
        V((hh, C), bf16), V((hh, C), bf16),
        V((PIECES, n1, 128), bf16), V((PIECES, M - 1, n2, 128), bf16), V(r3, bf16),
        D((5,)), D((5,)), D((M - 1, CHUNKS)), D((M - 1, CHUNKS)), D((5,)), D((5,)),
        D((PIECES,)), D((PIECES,)), D((PIECES, M - 1)), D((PIECES, M - 1)), D((PIECES, L - 1)), D((PIECES, L - 1)),
        D((PIECES, L - 1)), D((PIECES, L - 1)), D((PIECES, M - 1)), D((PIECES, M - 1)), D((PIECES,)), D((PIECES,)),
    ]
    spec = pl.BlockSpec(memory_space=pltpu.VMEM)
    far = pl.BlockSpec(memory_space=pltpu.HBM)
    gl, gc, go = pl.pallas_call(
        functools.partial(kernel, sizes),
        out_shape=(jax.ShapeDtypeStruct((n, C), bf16), jax.ShapeDtypeStruct((K * C, C), f32),
                   jax.ShapeDtypeStruct((fields, C), f32)),
        in_specs=[pl.BlockSpec(memory_space=pltpu.SMEM), far, far, spec, far, spec],
        out_specs=(spec,) * 3,
        scratch_shapes=scratch,
        compiler_params=pltpu.CompilerParams(
            collective_id=0, has_side_effects=True, vmem_limit_bytes=63 * 1024 * 1024),
    )(widths, latent.reshape(n, C), target.reshape(n, fields), q2, conv_weight, output_weight.T)
    return gl.reshape(1, rows, cols, C), gc, go.T


def solution(mesh):
    in_specs = (
        P(("groups", "member"), "lat", "lon", None),
        P(("groups", "lat"), "lon", None),
        P(),
        P(),
        P(),
        P(),
    )
    out_specs = (P(("groups", "member"), "lat", "lon", None), P("groups", None), P("groups", None))
    body = functools.partial(local, dict(mesh.shape))
    return jax.shard_map(body, mesh=mesh, in_specs=in_specs, out_specs=out_specs, check_vma=False)
```

```python
import functools
import math

import jax
import jax.numpy as jnp
from jax import lax
from jax.experimental import pallas as pl
from jax.experimental.pallas import tpu as pltpu
from jax.sharding import PartitionSpec as P

smoothing = 0.1
MESH = pl.DeviceIdType.MESH
f32 = jnp.float32
bf16 = jnp.bfloat16
CHUNKS = 4
PIECES = 3


def slope(d):
    return d * lax.rsqrt(d * d + smoothing * smoothing)


def dims_of(rows, cols, taps_lat, half):
    pitch = cols + 2 * half
    slots = rows + taps_lat - 1
    window = -(-(16 + taps_lat * pitch) // 128) * 128
    return pitch, slots, window, (rows - 1) * pitch + window


def kernel(sizes, wid_ref, lat_hbm, tgt_hbm, q_ref, cw_hbm, ow_ref, gl_ref, gc_ref, go_ref,
           lat_ref, tgt_ref, cw_ref, ins, base, FP, T, X, G, basis, BG, DG, mixed, F, FR, wo, pg, hg, GF, GB, GA,
           SL, SR, RL, RR, RC, SL2, SR2, SC2, QL, QR, QC, QLd, QRd, R1, R2, R3,
           hs, hr, fs, fr, as_, ar, s1s, s1r, s2s, s2r, s3s, s3r, a3s, a3r, a2s, a2r, a1s, a1r):
    rows, cols, C, K, taps_lat, half, L, M, fields, scale = sizes
    radius = taps_lat // 2
    pitch, slots, window, span = dims_of(rows, cols, taps_lat, half)
    n = rows * cols
    per = rows // CHUNKS
    cn = per * cols
    lat = lax.axis_index("lat")
    lon = lax.axis_index("lon")
    mem = lax.axis_index("member")
    other = 1 - lat
    right = lax.rem(lon + 1, L)
    left = lax.rem(lon + L - 1, L)
    hh = radius * half

    def rcopy(src, dst, ss, rs, dev):
        return pltpu.make_async_remote_copy(
            src_ref=src, dst_ref=dst, send_sem=ss, recv_sem=rs, device_id=dev, device_id_type=MESH)

    loads = [pltpu.make_async_copy(src, dst, ins.at[i]) for i, (src, dst) in enumerate(
        [(lat_hbm, lat_ref), (cw_hbm, cw_ref), (tgt_hbm, tgt_ref)])]
    for c in loads:
        c.start()
    barrier = pltpu.get_barrier_semaphore()
    peers = [{"lat": other}, {"lat": other, "lon": left}, {"lat": other, "lon": right}]
    peers += [{"lon": lax.rem(lon + d, L)} for d in range(1, L)]
    peers += [{"member": lax.rem(mem + d, M)} for d in range(1, M)]
    for dev in peers:
        pl.semaphore_signal(barrier, inc=1, device_id=dev, device_id_type=MESH)

    loads[0].wait()
    lat3 = lat_ref[...].astype(f32).reshape(rows, cols, C)
    SL[...] = lat3[:, :half].reshape(rows * half, C).astype(bf16)
    SR[...] = lat3[:, cols - half:].reshape(rows * half, C).astype(bf16)
    zero_halo = jnp.zeros((hh, C), bf16)
    edge = pl.multiple_of(lat * (hh + rows * half), 16)
    RL[pl.ds(edge, hh), :] = zero_halo
    RR[pl.ds(edge, hh), :] = zero_halo
    pl.semaphore_wait(barrier, len(peers))

    near = pl.multiple_of(other * (rows - radius) * half, 16)
    far = pl.multiple_of(lat * 0 + (1 - other) * (hh + rows * half), 16)
    nearrow = pl.multiple_of(other * (rows - radius) * cols, 16)
    inner = pl.ds(hh, rows * half)
    halo = [
        rcopy(SL, RR.at[inner], hs.at[0], hr.at[0], {"lon": left}),
        rcopy(SR, RL.at[inner], hs.at[1], hr.at[1], {"lon": right}),
        rcopy(SL.at[pl.ds(near, hh)], RR.at[pl.ds(far, hh)], hs.at[2], hr.at[2], {"lat": other, "lon": left}),
        rcopy(SR.at[pl.ds(near, hh)], RL.at[pl.ds(far, hh)], hs.at[3], hr.at[3], {"lat": other, "lon": right}),
        rcopy(lat_ref.at[pl.ds(nearrow, radius * cols)], RC, hs.at[4], hr.at[4], {"lat": other}),
    ]
    for c in halo:
        c.start()

    taps = q_ref.shape[0]
    taps_lon = taps // taps_lat
    nlat = 2 * rows
    tap = lax.broadcasted_iota(jnp.int32, (taps, window), 0)
    lane = lax.broadcasted_iota(jnp.int32, (taps, window), 1) - (16 - half)
    tap_a = tap // taps_lon
    place = (lane == tap_a * pitch + (tap - tap_a * taps_lon)).astype(bf16)
    base[...] = lax.dot_general(q_ref[...], place, (((0,), (0,)), ((), ())), preferred_element_type=f32)
    lane1 = lax.broadcasted_iota(jnp.int32, (1, window), 1) - (16 - half)
    offset = jnp.abs(lane1 - lane1 // pitch * pitch - half)

    def build(i, carry):
        row = lat * rows + i
        keep = offset <= wid_ref[row]
        for k in range(K):
            line = jnp.where(keep, base[pl.ds(k * nlat + row, 1), :], 0.0)
            line = jnp.broadcast_to(line, (cols, window))
            T[i, k * cols:(k + 1) * cols, :] = pltpu.roll(line, 0, 1, stride=1, stride_axis=0).astype(bf16)
        return carry
    lax.fori_loop(0, rows, build, 0)

    G[...] = jnp.zeros(G.shape, f32)
    wo[...] = jnp.concatenate([ow_ref[...].astype(f32), jnp.zeros((128 - fields, C), f32)], axis=0).astype(bf16)
    pg[...] = jnp.zeros(pg.shape, bf16)
    X[pl.ds(16 + slots * pitch, span - 16 - slots * pitch), :] = jnp.zeros((span - 16 - slots * pitch, C), bf16)
    for r in range(rows):
        X[16 + pitch * (r + radius):16 + pitch * (r + radius) + cols, :] = lat_ref[r * cols:(r + 1) * cols, :]
    zrow = jnp.zeros((cols, C), bf16)
    for r in range(radius):
        X[pl.ds(pl.multiple_of(16 + pitch * (r + lat * (rows + radius)), 16), cols), :] = zrow
    for c in halo:
        c.wait()
    for r in range(radius):
        X[pl.ds(pl.multiple_of(16 + pitch * (r + other * (rows + radius)), 16), cols), :] = RC[r * cols:(r + 1) * cols, :]
    rl = RL[...].astype(f32)
    rr = RR[...].astype(f32)
    z8 = jnp.zeros((half, C), f32)
    X[0:16, :] = jnp.concatenate([z8, rl[0:half]], axis=0).astype(bf16)
    for r in range(slots):
        nxt = rl[(r + 1) * half:(r + 2) * half] if r + 1 < slots else z8
        X[16 + pitch * r + cols:16 + pitch * (r + 1), :] = jnp.concatenate(
            [rr[r * half:(r + 1) * half], nxt], axis=0).astype(bf16)

    loads[1].wait()
    loads[2].wait()
    c0 = math.sqrt(2 / math.pi)
    groups = cn // 16
    lw = fields - 64
    assert groups * lw == 128
    pn = cn // 2 + 16
    fcopies = []
    for ch in range(CHUNKS):
        def conv(ii, carry, ch=ch):
            i = ch * per + ii
            out = jnp.dot(T[i], X[pl.ds(pl.multiple_of(i * pitch, 16), window), :], preferred_element_type=f32).astype(bf16)
            for k in range(K):
                basis[pl.ds(pl.multiple_of(i * cols, 16), cols), k * C:(k + 1) * C] = out[k * cols:(k + 1) * cols]
            return carry
        lax.fori_loop(0, per, conv, 0, unroll=True)
        sl = slice(ch * cn, (ch + 1) * cn)
        h = jnp.dot(basis[sl, :], cw_ref[...], preferred_element_type=f32)
        t = jnp.tanh(c0 * (h + 0.044715 * h * h * h))
        DG[sl, :] = 0.5 * (1 + t) + 0.5 * h * (1 - t * t) * (c0 * (1 + 3 * 0.044715 * h * h))
        mx = (lat_ref[sl, :].astype(f32) + 0.5 * h * (1 + t)).astype(bf16)
        mixed[sl, :] = mx
        fc = lax.dot_general(mx, wo[...], (((1,), (1,)), ((), ())), preferred_element_type=f32)
        F[sl, :] = fc.astype(bf16)
        psl = pl.ds(ch * pn, pn)
        both = jnp.concatenate([fc[:cn // 2, :64], fc[cn // 2:, :64]], axis=1)
        rest = jnp.concatenate([fc[g * 16:(g + 1) * 16, 64:fields] for g in range(groups)], axis=1)
        FP[ch * pn:(ch + 1) * pn, :] = jnp.concatenate([both, rest], axis=0).astype(bf16)
        cs = []
        for d in range(1, M):
            c = rcopy(FP.at[psl], FR.at[d - 1, psl], fs.at[d - 1, ch], fr.at[d - 1, ch],
                      {"member": lax.rem(mem + d, M)})
            c.start()
            cs.append(c)
        fcopies.append(cs)

    for ch in range(CHUNKS):
        sl = slice(ch * cn, (ch + 1) * cn)
        mine = F[sl, :fields].astype(f32)
        first = slope(mine - tgt_ref[sl, :])
        for c in fcopies[ch]:
            c.wait()
        pair = jnp.zeros_like(mine)
        for d in range(1, M):
            got = FR[d - 1, ch * pn:(ch + 1) * pn, :].astype(f32)
            body = got[:cn // 2]
            rest = got[cn // 2:]
            theirs = jnp.concatenate([
                jnp.concatenate([body[:, :64], body[:, 64:]], axis=0),
                jnp.concatenate([rest[:, g * lw:(g + 1) * lw] for g in range(groups)], axis=0)], axis=1)
            pair = pair + slope(mine - theirs)
        pg[sl, :fields] = (first - pair * (1.0 / (M - 1))).astype(bf16)
        up = jnp.dot(pg[sl, :], wo[...], preferred_element_type=f32)
        for ii in range(per):
            r = ch * per + ii + radius
            G[16 + pitch * r:16 + pitch * r + cols, :] = up[ii * cols:(ii + 1) * cols]
        hg[sl, :] = (up * DG[sl, :]).astype(bf16)

    KC = K * C
    hc = C // 2
    total = 2 * KC + 256
    tc = total // PIECES
    n1 = tc // 2
    n2 = n1 // M
    scatter = n2 % (16 * L) == 0
    n3 = n2 // L if scatter else n2
    o1 = [pl.multiple_of(c * tc + lat * n1, 16) for c in range(PIECES)]
    o1o = [pl.multiple_of(c * tc + other * n1, 16) for c in range(PIECES)]
    o2 = [pl.multiple_of(o1[c] + mem * n2, 16) for c in range(PIECES)]
    tn = (((0,), (0,)), ((), ()))
    st1 = []

    def ready(done):
        while len(st1) < PIECES and (len(st1) + 1) * tc <= done:
            c = len(st1)
            copy = rcopy(GB.at[pl.ds(o1o[c], n1)], R1.at[c], s1s.at[c], s1r.at[c], {"lat": other})
            copy.start()
            st1.append(copy)

    hgv = hg[...]
    for k in range(K):
        g = lax.dot_general(basis[:, k * C:(k + 1) * C], hgv, tn, preferred_element_type=f32)
        for half_id in range(2):
            part = g[:, half_id * hc:(half_id + 1) * hc]
            at = (2 * k + half_id) * C
            GF[at:at + C, :] = part
            GB[at:at + C, :] = part.astype(bf16)
        ready(2 * (k + 1) * C)
    g = lax.dot_general(pg[...], mixed[...], tn, preferred_element_type=f32)
    for half_id in range(2):
        part = g[:, half_id * hc:(half_id + 1) * hc]
        at = 2 * KC + half_id * 128
        GF[at:at + 128, :] = part
        GB[at:at + 128, :] = part.astype(bf16)
    ready(total)

    def adjoint(first_row, last_row):
        lo, size = first_row * cols, (last_row - first_row) * cols
        BG[lo:lo + size, :] = lax.dot_general(
            hg[lo:lo + size, :], cw_ref[...], (((1,), (1,)), ((), ())), preferred_element_type=f32).astype(bf16)

        def body(i, carry):
            at = pl.ds(pl.multiple_of(i * cols, 16), cols)
            stacked = jnp.concatenate([BG[at, k * C:(k + 1) * C] for k in range(K)], axis=0)
            out = lax.dot_general(T[i], stacked, tn, preferred_element_type=f32)
            w = pl.ds(pl.multiple_of(i * pitch, 16), window)
            G[w, :] = G[w, :] + out
            return carry
        lax.fori_loop(first_row, last_row, body, 0)

    quarter = rows // 4
    adjoint(0, quarter)
    st2 = []
    for c in range(PIECES):
        st1[c].wait()
        w = pl.ds(o1[c], n1)
        v = GF[w, :] + R1[c].astype(f32)
        GF[w, :] = v
        GB[w, :] = v.astype(bf16)
        cs = []
        for d in range(1, M):
            q = lax.rem(mem + d, M)
            copy = rcopy(GB.at[pl.ds(pl.multiple_of(o1[c] + q * n2, 16), n2)], R2.at[c, d - 1],
                         s2s.at[c, d - 1], s2r.at[c, d - 1], {"member": q})
            copy.start()
            cs.append(copy)
        st2.append(cs)

    st3 = []
    for c in range(PIECES):
        adjoint((c + 1) * quarter, (c + 2) * quarter)
        for copy in st2[c]:
            copy.wait()
        w = pl.ds(o2[c], n2)
        v = GF[w, :]
        for d in range(1, M):
            v = v + R2[c, d - 1].astype(f32)
        GF[w, :] = v
        GB[w, :] = v.astype(bf16)
        cs = []
        for d in range(1, L):
            q = lax.rem(lon + d, L)
            src = GB.at[pl.ds(pl.multiple_of(o2[c] + q * n3, 16), n3)] if scatter else GB.at[w]
            dst = R3.at[c, d - 1] if scatter else R3.at[c, lon]
            copy = rcopy(src, dst, s3s.at[c, d - 1], s3r.at[c, d - 1], {"lon": q})
            copy.start()
            cs.append(copy)
        st3.append(cs)

    SR2[...] = jnp.concatenate([G[16 + pitch * r + cols:16 + pitch * r + cols + half, :] for r in range(slots)], axis=0).astype(bf16)
    SL2[...] = jnp.concatenate([G[16 + pitch * r - half:16 + pitch * r, :] for r in range(slots)], axis=0).astype(bf16)
    for r in range(radius):
        SC2[r * cols:(r + 1) * cols, :] = G[pl.ds(pl.multiple_of(16 + pitch * (r + other * (rows + radius)), 16), cols), :].astype(bf16)
    beyond = pl.multiple_of(other * (hh + rows * half), 16)
    back = [
        rcopy(SR2.at[inner], QL, as_.at[0], ar.at[0], {"lon": right}),
        rcopy(SL2.at[inner], QR, as_.at[1], ar.at[1], {"lon": left}),
        rcopy(SR2.at[pl.ds(beyond, hh)], QLd, as_.at[2], ar.at[2], {"lat": other, "lon": right}),
        rcopy(SL2.at[pl.ds(beyond, hh)], QRd, as_.at[3], ar.at[3], {"lat": other, "lon": left}),
        rcopy(SC2, QC, as_.at[4], ar.at[4], {"lat": other}),
    ]
    for c in back:
        c.start()

    ag3 = []
    for c in range(PIECES):
        for copy in st3[c]:
            copy.wait()
        cs = []
        if scatter:
            w = pl.ds(pl.multiple_of(o2[c] + lon * n3, 16), n3)
            v = GF[w, :]
            for d in range(1, L):
                v = v + R3[c, d - 1].astype(f32)
            GA[w, :] = v.astype(bf16)
            for d in range(1, L):
                copy = rcopy(GA.at[w], GA.at[w], a3s.at[c, d - 1], a3r.at[c, d - 1], {"lon": lax.rem(lon + d, L)})
                copy.start()
                cs.append(copy)
        else:
            w = pl.ds(o2[c], n2)
            R3[c, lon] = GB[w, :]
            v = R3[c, 0].astype(f32)
            for q in range(1, L):
                v = v + R3[c, q].astype(f32)
            GA[w, :] = v.astype(bf16)
        ag3.append(cs)

    ag2 = []
    for c in range(PIECES):
        for copy in ag3[c]:
            copy.wait()
        w = pl.ds(o2[c], n2)
        cs = []
        for d in range(1, M):
            copy = rcopy(GA.at[w], GA.at[w], a2s.at[c, d - 1], a2r.at[c, d - 1], {"member": lax.rem(mem + d, M)})
            copy.start()
            cs.append(copy)
        ag2.append(cs)
    for c in back:
        c.wait()
    ql = QL[...].astype(f32)
    qr = QR[...].astype(f32)
    qld = QLd[...].astype(f32)
    qrd = QRd[...].astype(f32)
    for r in range(rows):
        at = 16 + pitch * (r + radius)
        G[at:at + half, :] = G[at:at + half, :] + ql[r * half:(r + 1) * half]
        G[at + cols - half:at + cols, :] = G[at + cols - half:at + cols, :] + qr[r * half:(r + 1) * half]
    for r in range(radius):
        at = 16 + pitch * (radius + r + other * (rows - radius))
        w = pl.ds(pl.multiple_of(at, 16), cols)
        G[w, :] = G[w, :] + QC[r * cols:(r + 1) * cols, :].astype(f32)
        w = pl.ds(pl.multiple_of(at, 8), half)
        G[w, :] = G[w, :] + qld[r * half:(r + 1) * half]
        w = pl.ds(pl.multiple_of(at + cols - half, 8), half)
        G[w, :] = G[w, :] + qrd[r * half:(r + 1) * half]
    for r in range(rows):
        at = 16 + pitch * (r + radius)
        gl_ref[r * cols:(r + 1) * cols, :] = G[at:at + cols, :].astype(bf16)

    ag1 = []
    for c in range(PIECES):
        for copy in ag2[c]:
            copy.wait()
        w = pl.ds(o1[c], n1)
        copy = rcopy(GA.at[w], GA.at[w], a1s.at[c], a1r.at[c], {"lat": other})
        copy.start()
        ag1.append(copy)
    block = 0
    for c in range(PIECES):
        ag1[c].wait()
        while block < 2 * K and (block + 1) * C <= (c + 1) * tc:
            k, half_id = block // 2, block % 2
            gc_ref[k * C:(k + 1) * C, half_id * hc:(half_id + 1) * hc] = GA[block * C:(block + 1) * C, :].astype(f32) * scale
            block += 1
    for half_id in range(2):
        at = 2 * KC + half_id * 128
        go_ref[:, half_id * hc:(half_id + 1) * hc] = GA[at:at + 128, :].astype(f32)[:fields] * scale


def local(mesh_shape, latent, target, quadrature, widths, conv_weight, output_weight):
    rows, cols, C = latent.shape[1:]
    K, _, taps_lat, taps_lon = quadrature.shape
    half = taps_lon // 2
    fields = output_weight.shape[1]
    L, M = mesh_shape["lon"], mesh_shape["member"]
    lats = mesh_shape["lat"]
    assert lats == 2
    pitch, slots, window, span = dims_of(rows, cols, taps_lat, half)
    n = rows * cols
    radius = taps_lat // 2
    hh = radius * half
    q2 = quadrature.transpose(2, 3, 0, 1).reshape(taps_lat * taps_lon, K * rows * lats)
    scale = 1.0 / math.sqrt(M * rows * lats * cols * L)
    sizes = (rows, cols, C, K, taps_lat, half, L, M, fields, scale)
    total = 2 * K * C + 256
    n1 = total // PIECES // 2
    n2 = n1 // M
    scatter = n2 % (16 * L) == 0
    r3 = (PIECES, L - 1, n2 // L, 128) if scatter else (PIECES, L, n2, 128)
    pn = n // CHUNKS // 2 + 16
    V = pltpu.VMEM
    D = pltpu.SemaphoreType.DMA
    scratch = [
        V((n, C), bf16), V((n, fields), f32), V((K * C, C), bf16), D((3,)),
        V((K * rows * lats, window), f32), V((CHUNKS * pn, 128), bf16),
        V((rows, K * cols, window), bf16), V((span, C), bf16), V((span, C), f32),
        V((n, K * C), bf16), V((n, K * C), bf16), V((n, C), f32), V((n, C), bf16),
        V((n, 128), bf16), V((M - 1, CHUNKS * pn, 128), bf16), V((128, C), bf16), V((n, 128), bf16), V((n, C), bf16),
        V((total, 128), f32), V((total, 128), bf16), V((total, 128), bf16),
        V((rows * half, C), bf16), V((rows * half, C), bf16),
        V((slots * half, C), bf16), V((slots * half, C), bf16), V((radius * cols, C), bf16),
        V((slots * half, C), bf16), V((slots * half, C), bf16), V((radius * cols, C), bf16),
        V((rows * half, C), bf16), V((rows * half, C), bf16), V((radius * cols, C), bf16),
        V((hh, C), bf16), V((hh, C), bf16),
        V((PIECES, n1, 128), bf16), V((PIECES, M - 1, n2, 128), bf16), V(r3, bf16),
        D((5,)), D((5,)), D((M - 1, CHUNKS)), D((M - 1, CHUNKS)), D((5,)), D((5,)),
        D((PIECES,)), D((PIECES,)), D((PIECES, M - 1)), D((PIECES, M - 1)), D((PIECES, L - 1)), D((PIECES, L - 1)),
        D((PIECES, L - 1)), D((PIECES, L - 1)), D((PIECES, M - 1)), D((PIECES, M - 1)), D((PIECES,)), D((PIECES,)),
    ]
    spec = pl.BlockSpec(memory_space=pltpu.VMEM)
    far = pl.BlockSpec(memory_space=pltpu.HBM)
    gl, gc, go = pl.pallas_call(
        functools.partial(kernel, sizes),
        out_shape=(jax.ShapeDtypeStruct((n, C), bf16), jax.ShapeDtypeStruct((K * C, C), f32),
                   jax.ShapeDtypeStruct((fields, C), f32)),
        in_specs=[pl.BlockSpec(memory_space=pltpu.SMEM), far, far, spec, far, spec],
        out_specs=(spec,) * 3,
        scratch_shapes=scratch,
        compiler_params=pltpu.CompilerParams(
            collective_id=0, has_side_effects=True, vmem_limit_bytes=63 * 1024 * 1024),
    )(widths, latent.reshape(n, C), target.reshape(n, fields), q2, conv_weight, output_weight.T)
    return gl.reshape(1, rows, cols, C), gc, go.T


def solution(mesh):
    in_specs = (
        P(("groups", "member"), "lat", "lon", None),
        P(("groups", "lat"), "lon", None),
        P(),
        P(),
        P(),
        P(),
    )
    out_specs = (P(("groups", "member"), "lat", "lon", None), P("groups", None), P("groups", None))
    body = functools.partial(local, dict(mesh.shape))
    return jax.shard_map(body, mesh=mesh, in_specs=in_specs, out_specs=out_specs, check_vma=False)
```
